32 devices in a mesh: gx: 8 (over y, x, core), gy: 4 (over z).
Axes of the slice: x: 2, y: 2, z: 4, core: 2. Of those that a mesh axis runs over, the one named last changes fastest.
Arguments:
- held_head: float32 [4096, 8, 128], P(('gx', 'gy')), may hold values from -6 to -0.5
- held_head_old: float32 [4096, 8, 128], P(('gx', 'gy')), may hold values from -6 to -0.5
- material_ids: int32 [128, 64, 512], P(None, 'gx', 'gy'), may hold values from 0 to 15
- block_map: int32 [32, 32], replicated, may hold values from 0 to 31, as said below
- conductivity: float32 [3, 16], replicated, may hold values from 0.1 to 10
- vg_alpha: float32 [16], replicated, may hold values from 0.5 to 4
- vg_n: float32 [16], replicated, may hold values from 1.5 to 3
- capacity: float32 [16], replicated, may hold values from 0.1 to 0.45
Outputs:
- update: float32 [128, 64, 512], P(None, 'gx', 'gy')
The draws below stay inside these ranges and needn't reach their ends.
Inputs may be any that keep to these rules, and one draw needn't show every extreme that they name: Every row and every column of block_map holds each brick number once.
All inputs are finite; a program needn't handle non-finite values.
Results may differ from the reference program's by a relative error of at most 0.0001.
Values sent between devices are 32-bit elements; how exact they have to be, the bound alone decides.
A program may use at most 128 MiB of HBM per device.

```python
import math
import jax
import jax.numpy as jnp
from jax import lax

CX = 8
CY = 128
NZ = 128
MATERIALS = 16
ITERS = 4
BRICKS = 32
NX = 64
NY = 512
SLAB = 4
N_GX = 8
N_GY = 4


def draw_block_map(key, part):
    first_key = jax.random.fold_in(key, 11)
    second_key = jax.random.fold_in(key, 12)
    third_key = jax.random.fold_in(key, 13)
    row_shift = jax.random.permutation(first_key, BRICKS)
    column_shift = jax.random.permutation(second_key, BRICKS)
    relabel = jax.random.permutation(third_key, BRICKS)
    square = (row_shift[:, None] + column_shift[None, :]) % BRICKS
    return relabel[square].astype(jnp.int32)


def place_ends(drawn, rng, smallest, top_value):
    spot = [jax.random.randint(jax.random.fold_in(rng, axis), (), 0, length) for axis, length in enumerate(drawn.shape)]
    longest = drawn.shape.index(max(drawn.shape))
    neighbour = spot[:longest] + [(spot[longest] + 1) % drawn.shape[longest]] + spot[longest + 1:]
    return drawn.at[tuple(spot)].set(smallest).at[tuple(neighbour)].set(top_value)


def shard_levels(stream_key, dims, split, low, top_value):
    def one(dim, parts):
        steps = jax.random.uniform(jax.random.fold_in(jax.random.fold_in(stream_key, 6), dim), (parts,), jnp.float32, low / len(split), top_value / len(split))
        return jnp.repeat(jnp.exp(steps), dims[dim] // parts).reshape((-1,) + (1,) * (len(dims) - dim - 1))

    factor_of = one(*split[0])
    for cut in split[1:]:
        factor_of = factor_of * one(*cut)
    return factor_of


def setup_inputs(seed: int = 0) -> dict:
    keys = jax.random.split(jax.random.key(seed), 9)
    return {
        "held_head": jnp.clip(-6.0 + 5.5 * jax.random.uniform(keys[0], (BRICKS * NZ, CX, CY), jnp.float32) ** shard_levels(keys[0], (BRICKS * NZ, CX, CY), ((0, 32),), -0.2, 0.2), -6.0, -0.5),
        "held_head_old": jnp.clip(-6.0 + 5.5 * jax.random.uniform(keys[1], (BRICKS * NZ, CX, CY), jnp.float32) ** shard_levels(keys[1], (BRICKS * NZ, CX, CY), ((0, 32),), -0.2, 0.2), -6.0, -0.5),
        "material_ids": place_ends(jax.random.randint(keys[2], (NZ, NX, NY), 0, MATERIALS), jax.random.fold_in(keys[2], 1), 0, MATERIALS - 1).astype(jnp.int32),
        "block_map": draw_block_map(jax.random.fold_in(keys[8], 71), 0),
        "conductivity": jnp.clip(jnp.exp(jax.random.uniform(keys[4], (3, MATERIALS), jnp.float32, math.log(0.1), math.log(10.0))), 0.1, 10.0),
        "vg_alpha": jnp.clip(jnp.exp(jax.random.uniform(keys[5], (MATERIALS,), jnp.float32, math.log(0.5), math.log(4.0))), 0.5, 4.0),
        "vg_n": jnp.clip(jax.random.uniform(keys[6], (MATERIALS,), jnp.float32, 1.5, 3.0), 1.5, 3.0),
        "capacity": jnp.clip(jax.random.uniform(keys[7], (MATERIALS,), jnp.float32, 0.1, 0.45), 0.1, 0.45),
    }


STORE = 4.0

def retention(level, alpha_cell, expo_cell):
    scaled = alpha_cell * -level
    power = jnp.exp(expo_cell * jnp.log(scaled))
    exponent = 1.0 - 1.0 / expo_cell
    inverse = 1.0 / (1.0 + power)
    saturation = jnp.exp(exponent * jnp.log(inverse))
    inner_term = -jnp.expm1(exponent * jnp.log1p(-inverse))
    relperm = jnp.sqrt(saturation) * inner_term * inner_term
    return (saturation, relperm)

def properties(material_ids, conductivity, vg_alpha, vg_n, capacity):
    blank = jnp.zeros(material_ids.shape, conductivity.dtype)
    fields = [blank, blank, blank, blank, blank, blank]
    for m in range(MATERIALS):
        match_cell = material_ids == m
        values = (conductivity[0, m], conductivity[1, m], conductivity[2, m], vg_alpha[m], vg_n[m], capacity[m])
        fields = [jnp.where(match_cell, value, field) for value, field in zip(values, fields)]
    return fields

def pair_slices(padded, axis):
    lower_index = [slice(1, -1), slice(1, -1), slice(1, -1)]
    higher_index = [slice(1, -1), slice(1, -1), slice(1, -1)]
    lower_index[axis] = slice(0, -1)
    higher_index[axis] = slice(1, None)
    return (padded[tuple(lower_index)], padded[tuple(higher_index)])

def face_terms(pad_head, pad_rel, pad_cond, axis, rise):
    head_low, head_high = pair_slices(pad_head, axis)
    rel_low, rel_high = pair_slices(pad_rel, axis)
    cond_low, cond_high = pair_slices(pad_cond, axis)
    trans = 2.0 * cond_low * cond_high / (cond_low + cond_high)
    potential = head_high - head_low + rise
    along = trans * (0.5 * (rel_low + rel_high))
    slope = trans * potential * 0.5
    return (along, slope, along * potential)

def net_inflow(flux, axis):
    extent = flux.shape[axis]
    return lax.slice_in_dim(flux, 1, extent, axis=axis) - lax.slice_in_dim(flux, 0, extent - 1, axis=axis)

def least_squares(hess, beta):
    matrix_rows = [hess[i] for i in range(ITERS + 1)]
    target = [beta] + [jnp.zeros_like(beta) for i in range(ITERS)]
    for j in range(ITERS):
        first = matrix_rows[j][j]
        second = matrix_rows[j + 1][j]
        radius = jnp.sqrt(first * first + second * second)
        cosine = first / radius
        sine_value = second / radius
        row_top, row_next = (matrix_rows[j], matrix_rows[j + 1])
        matrix_rows[j] = cosine * row_top + sine_value * row_next
        matrix_rows[j + 1] = cosine * row_next - sine_value * row_top
        goal_top, goal_next = (target[j], target[j + 1])
        target[j] = cosine * goal_top + sine_value * goal_next
        target[j + 1] = cosine * goal_next - sine_value * goal_top
    coeffs = [None] * ITERS
    for j in reversed(range(ITERS)):
        running = target[j]
        for k in range(j + 1, ITERS):
            running = running - matrix_rows[j][k] * coeffs[k]
        coeffs[j] = running / matrix_rows[j][j]
    return coeffs

def reference(held_head, held_head_old, material_ids, block_map, conductivity, vg_alpha, vg_n, capacity):
    global_map = block_map.astype(jnp.int32)
    numbers = jnp.arange(BRICKS, dtype=jnp.int32)
    holder = lax.optimization_barrier(jnp.sum(jnp.where(global_map[None, :, :] == numbers[:, None, None], numbers[None, :, None], 0), axis=1))

    def relay_one(held):
        pieces = held.reshape((BRICKS, BRICKS, SLAB, CX, CY))
        bricks = pieces[holder, numbers[None, :]]
        bricks = bricks.reshape((N_GX, N_GY, NZ, CX, CY))
        return jnp.transpose(bricks, (2, 0, 3, 1, 4)).reshape((NZ, NX, NY))
    head = relay_one(held_head)
    head_old = relay_one(held_head_old)
    cond_x, cond_y, cond_z, alpha_cell, expo_cell, cap_cell = properties(material_ids, conductivity, vg_alpha, vg_n, capacity)
    ones_field = jnp.ones_like(head)
    (saturation, relperm), (d_sat, d_rel) = jax.jvp(lambda level: retention(level, alpha_cell, expo_cell), (head,), (ones_field,))
    old_sat = retention(head_old, alpha_cell, expo_cell)[0]
    pad_head = jnp.pad(head, 1)
    pad_rel = jnp.pad(relperm, 1)
    pad_drel = jnp.pad(d_rel, 1)
    layout = [(1, jnp.pad(cond_x, 1), 0.0), (2, jnp.pad(cond_y, 1), 0.0), (0, jnp.pad(cond_z, 1), 1.0)]
    coefficients = []
    total_in = None
    for axis, pad_cond, rise in layout:
        along, slope, flux = face_terms(pad_head, pad_rel, pad_cond, axis, rise)
        coefficients.append((axis, along, slope))
        inflow = net_inflow(flux, axis)
        total_in = inflow if total_in is None else total_in + inflow
    newton_residual = STORE * cap_cell * (saturation - old_sat) - total_in
    diagonal = STORE * cap_cell * d_sat

    def apply_jacobian(field):
        pad_field = jnp.pad(field, 1)
        pad_weighted = pad_drel * pad_field
        total_change = None
        for axis, along, slope in coefficients:
            field_low, field_high = pair_slices(pad_field, axis)
            weight_low, weight_high = pair_slices(pad_weighted, axis)
            change = along * (field_high - field_low) + slope * (weight_low + weight_high)
            inflow = net_inflow(change, axis)
            total_change = inflow if total_change is None else total_change + inflow
        return diagonal * field - total_change
    start = -newton_residual
    beta = jnp.sqrt(jnp.sum(start * start))
    basis = [start / beta]
    hess = jnp.zeros((ITERS + 1, ITERS), newton_residual.dtype)
    for j in range(ITERS):
        image = apply_jacobian(basis[j])
        products = [jnp.sum(image * vector) for vector in basis]
        for k in range(j + 1):
            image = image - products[k] * basis[k]
        norm_value = jnp.sqrt(jnp.sum(image * image))
        for k in range(j + 1):
            hess = hess.at[k, j].set(products[k])
        hess = hess.at[j + 1, j].set(norm_value)
        if j + 1 < ITERS:
            basis.append(image / norm_value)
    coeffs = least_squares(hess, beta)
    update = coeffs[0] * basis[0]
    for k in range(1, ITERS):
        update = update + coeffs[k] * basis[k]
    return update
```

```python
import functools

import jax
import jax.numpy as jnp
from jax import lax
from jax.experimental import pallas as pl
from jax.experimental.pallas import tpu as pltpu
from jax.sharding import PartitionSpec as P

MATERIALS = 16
ITERS = 4
STORE = 4.0
MESH = pl.DeviceIdType.MESH
TILE = 8


def expm1_negative(t):
    series = 1.0 + t * (1.0 / 8.0)
    for k in (7.0, 6.0, 5.0, 4.0, 3.0, 2.0):
        series = 1.0 + t * (1.0 / k) * series
    return jnp.where(t > -0.4, t * series, jnp.exp(t) - 1.0)


def saturation_parts(level, alpha_cell, expo_cell):
    scaled = alpha_cell * -level
    power = jnp.exp(expo_cell * jnp.log(scaled))
    exponent = 1.0 - 1.0 / expo_cell
    inverse = 1.0 / (1.0 + power)
    return power, exponent, inverse, exponent * jnp.log(inverse)


def rotate(column, rotations):
    column = list(column)
    for i, (cosine, sine) in enumerate(rotations):
        top, low = column[i], column[i + 1]
        column[i] = cosine * top + sine * low
        column[i + 1] = cosine * low - sine * top
    return column


def kernel(
    n_gx,
    n_gy,
    slab,
    order_ref,
    cond_ref,
    alpha_ref,
    expo_ref,
    cap_ref,
    head_ref,
    old_ref,
    ids_ref,
    out_ref,
    packed,
    arrived,
    zorder,
    level,
    cond_x,
    cond_y,
    cond_z,
    alpha_f,
    expo_f,
    cap_f,
    trans,
    store_f,
    diag_f,
    coef,
    krylov,
    basis,
    rim_c_out,
    rim_c,
    rim_h_out,
    rim_h,
    rim_v_out,
    rim_v,
    red_out,
    red_in,
    a2a_send,
    a2a_recv,
    rim_send,
    rim_recv,
    red_send,
    red_recv,
):
    n = n_gx * n_gy
    nz = ids_ref.shape[0] // TILE
    ny = ids_ref.shape[1]
    gx, gy = lax.axis_index("gx"), lax.axis_index("gy")
    me = gx * n_gy + gy
    block = slab * TILE

    def coords(d):
        return (d // n_gy, d % n_gy)

    zero_tile = jnp.zeros((TILE, nz), jnp.float32)
    zero_face = jnp.zeros((ny, nz), jnp.float32)

    def y_edges(ref, index):
        ref[index + (pl.ds(0, TILE), slice(None))] = zero_tile
        ref[index + (pl.ds((ny + 1) * TILE, TILE), slice(None))] = zero_tile

    y_edges(cond_y, ())
    for f in range(3):
        y_edges(level, (f,))
    for k in range(ITERS):
        y_edges(krylov, (k,))
    for side in range(2):
        rim_c[side] = zero_face
        for f in range(3):
            rim_h[side, f] = zero_face
        for k in range(ITERS):
            rim_v[k, side] = zero_face

    barrier = pltpu.get_barrier_semaphore()

    def greet(t, carry):
        pl.semaphore_signal(
            barrier, inc=1, device_id=coords(lax.rem(me + t, n)), device_id_type=MESH
        )
        return carry

    lax.fori_loop(1, n, greet, 0)

    def pack(d, carry):
        source = order_ref[0, d]
        packed[d, pl.ds(0, block), :] = head_ref[source]
        packed[d, pl.ds(block, block), :] = old_ref[source]
        return carry

    lax.fori_loop(0, n, pack, 0)
    pl.semaphore_wait(barrier, n - 1)

    def send_block(t, carry):
        d = lax.rem(me + t, n)
        pltpu.make_async_remote_copy(
            packed.at[d], arrived.at[me], a2a_send, a2a_recv, device_id=coords(d), device_id_type=MESH
        ).start()
        return carry

    lax.fori_loop(1, n, send_block, 0)
    arrived[me] = packed[me]

    wanted = (gx > 0, gx < n_gx - 1, gy > 0, gy < n_gy - 1)
    opposite = (wanted[1], wanted[0], wanted[3], wanted[2])
    partner = ((gx - 1, gy), (gx + 1, gy), (gx, gy - 1), (gx, gy + 1))

    def rim_copies(slot, x_out, x_in, y_ref):
        first, last = pl.ds(TILE, TILE), pl.ds(ny * TILE, TILE)
        below, above = pl.ds(0, TILE), pl.ds((ny + 1) * TILE, TILE)
        ends = (
            (x_out.at[0], x_in.at[1]),
            (x_out.at[1], x_in.at[0]),
            (y_ref(first), y_ref(above)),
            (y_ref(last), y_ref(below)),
        )
        return [
            pltpu.make_async_remote_copy(
                source,
                target,
                rim_send.at[slot, i],
                rim_recv.at[slot, i],
                device_id=partner[i],
                device_id_type=MESH,
            )
            for i, (source, target) in enumerate(ends)
        ]

    def start(copies):
        for copy, go in zip(copies, wanted):
            pl.when(go)(copy.start)

    def finish_recv(copies):
        for copy, go in zip(copies, opposite):
            pl.when(go)(copy.wait_recv)

    def finish_send(copies):
        for copy, go in zip(copies, wanted):
            pl.when(go)(copy.wait_send)

    rows = 4
    chunk = rows * TILE

    def cells(ref, i, index=(), offset=0):
        at = pl.ds(pl.multiple_of(i * chunk + offset, TILE), chunk)
        return ref[index + (at, slice(None))].reshape(rows, TILE, nz)

    def put(ref, i, value, index=(), offset=0):
        at = pl.ds(pl.multiple_of(i * chunk + offset, TILE), chunk)
        ref[index + (at, slice(None))] = value.reshape(chunk, nz)

    chunks = ny // rows

    for x in range(TILE):
        ids = ids_ref[pl.ds(x, nz, stride=TILE), :].T
        kinds = [jnp.zeros(ids.shape, jnp.float32) for i in range(6)]
        for m in range(MATERIALS):
            match = ids == m
            values = (
                cond_ref[0, m],
                cond_ref[1, m],
                cond_ref[2, m],
                alpha_ref[m],
                expo_ref[m],
                cap_ref[m],
            )
            kinds = [jnp.where(match, value, kind) for value, kind in zip(values, kinds)]
        here = pl.ds(x, ny, stride=TILE)
        cond_x[here, :] = kinds[0]
        cond_y[pl.ds(TILE + x, ny, stride=TILE), :] = kinds[1]
        cond_z[here, :] = kinds[2]
        alpha_f[here, :] = kinds[3]
        expo_f[here, :] = kinds[4]
        cap_f[here, :] = kinds[5]

    rim_c_out[0] = cond_x[pl.ds(0, ny, stride=TILE), :]
    rim_c_out[1] = cond_x[pl.ds(TILE - 1, ny, stride=TILE), :]
    cond_copies = rim_copies(0, rim_c_out, rim_c, lambda at: cond_y.at[at])
    start(cond_copies)
    finish_recv(cond_copies)

    shape = (rows, TILE, nz)
    x_at = lax.broadcasted_iota(jnp.int32, shape, 1)
    z_at = lax.broadcasted_iota(jnp.int32, shape, 2)

    def rim_rows(ref, i, index):
        at = pl.ds(i * rows, rows)
        return jnp.broadcast_to(ref[index + (at, slice(None))].reshape(rows, 1, nz), shape)

    def x_pair(v, low_rim, high_rim):
        low = jnp.where(x_at == 0, low_rim, pltpu.roll(v, 1, 1))
        high = jnp.where(x_at == TILE - 1, high_rim, pltpu.roll(v, TILE - 1, 1))
        return low, high

    def z_pair(v):
        return pltpu.roll(v, 1, 2), pltpu.roll(v, nz - 1, 2)

    def mean(a, b):
        return 2.0 * a * b / (a + b)

    def transmissibility(i, carry):
        kx = cells(cond_x, i)
        low, high = x_pair(kx, rim_rows(rim_c, i, (0,)), rim_rows(rim_c, i, (1,)))
        put(trans, i, mean(low, kx), (0,))
        put(trans, i, mean(kx, high), (1,))
        ky = cells(cond_y, i, (), TILE)
        put(trans, i, mean(cells(cond_y, i), ky), (2,))
        put(trans, i, mean(ky, cells(cond_y, i, (), 2 * TILE)), (3,))
        kz = cells(cond_z, i)
        low, high = z_pair(kz)
        put(trans, i, jnp.where(z_at == 0, 0.0, mean(low, kz)), (4,))
        put(trans, i, jnp.where(z_at == nz - 1, 0.0, mean(kz, high)), (5,))
        return carry

    lax.fori_loop(0, chunks, transmissibility, 0)

    others = pl.ds(0, n - 1)
    arrival = pltpu.make_async_remote_copy(
        packed.at[others], arrived.at[others], a2a_send, a2a_recv, device_id=coords(lax.rem(me + 1, n)), device_id_type=MESH
    )
    arrival.wait_recv()

    def unpack(p, carry):
        source = order_ref[1, p]
        at = pl.ds(pl.multiple_of(p * block, TILE), block)
        both = arrived[source]
        zorder[0, at, :] = both[:block]
        zorder[1, at, :] = both[block:]
        return carry

    lax.fori_loop(0, n, unpack, 0)
    for x in range(TILE):
        level[0, pl.ds(TILE + x, ny, stride=TILE), :] = zorder[0, pl.ds(x, nz, stride=TILE), :].T
        store_f[pl.ds(x, ny, stride=TILE), :] = zorder[1, pl.ds(x, nz, stride=TILE), :].T

    def retention(i, carry):
        alpha_cell, expo_cell = cells(alpha_f, i), cells(expo_f, i)
        capacity = STORE * cells(cap_f, i)
        head = cells(level, i, (0,), TILE)
        power, exponent, inverse, log_sat = saturation_parts(head, alpha_cell, expo_cell)
        rest = power * inverse
        root = jnp.exp(0.5 * log_sat)
        saturation = root * root
        inner = -expm1_negative(exponent * jnp.log1p(-inverse))
        gain = (expo_cell - 1.0) / -head
        put(level, i, root * inner * inner, (1,), TILE)
        put(level, i, root * inner * gain * (0.5 * rest * inner + 2.0 * (1.0 - inner) * inverse), (2,), TILE)
        old = saturation_parts(cells(store_f, i), alpha_cell, expo_cell)
        put(store_f, i, capacity * (saturation - jnp.exp(old[3])))
        put(diag_f, i, capacity * saturation * rest * gain)
        return carry

    lax.fori_loop(0, chunks, retention, 0)
    for f in range(3):
        rim_h_out[0, f] = level[f, pl.ds(TILE, ny, stride=TILE), :]
        rim_h_out[1, f] = level[f, pl.ds(2 * TILE - 1, ny, stride=TILE), :]
    level_copies = rim_copies(1, rim_h_out, rim_h, lambda at: level.at[:, at])
    start(level_copies)
    finish_recv(level_copies)

    def assemble(i, carry):
        here = [cells(level, i, (f,), TILE) for f in range(3)]
        pairs = []
        sides = [
            x_pair(here[f], rim_rows(rim_h, i, (0, f)), rim_rows(rim_h, i, (1, f))) for f in range(3)
        ]
        pairs += [[s[0] for s in sides], [s[1] for s in sides]]
        pairs += [[cells(level, i, (f,), 2 * TILE * side) for f in range(3)] for side in range(2)]
        sides = [z_pair(here[f]) for f in range(3)]
        pairs += [[s[0] for s in sides], [s[1] for s in sides]]
        head, rel, drel = here
        total = -cells(store_f, i)
        centre = cells(diag_f, i)
        for face, (head_b, rel_b, drel_b) in enumerate(pairs):
            half = 0.5 * cells(trans, i, (face,))
            rise = 1.0 if face >= 4 else 0.0
            along = half * (rel + rel_b)
            if face % 2:
                potential = head_b - head + rise
                slope = half * potential
                total = total + along * potential
                centre = centre + along - slope * drel
                put(coef, i, -along - slope * drel_b, (1 + face,))
            else:
                potential = head - head_b + rise
                slope = half * potential
                total = total - along * potential
                centre = centre + along + slope * drel
                put(coef, i, slope * drel_b - along, (1 + face,))
        put(coef, i, centre, (0,))
        put(krylov, i, total, (0,), TILE)
        return carry

    lax.fori_loop(0, chunks, assemble, 0)

    def send_rims(k):
        rim_v_out[k, 0] = krylov[k, pl.ds(TILE, ny, stride=TILE), :]
        rim_v_out[k, 1] = krylov[k, pl.ds(2 * TILE - 1, ny, stride=TILE), :]
        copies = rim_copies(2 + k, rim_v_out.at[k], rim_v.at[k], lambda at: krylov.at[k, at])
        start(copies)
        return copies

    def fold(value):
        return jnp.sum(value, axis=0)

    none = jnp.zeros((TILE, nz), jnp.float32)

    def apply_stencil(k, i):
        v = cells(krylov, i, (k,), TILE)
        x_low, x_high = x_pair(v, rim_rows(rim_v, i, (k, 0)), rim_rows(rim_v, i, (k, 1)))
        z_low, z_high = z_pair(v)
        total = cells(coef, i, (0,)) * v
        total = total + cells(coef, i, (1,)) * x_low + cells(coef, i, (2,)) * x_high
        total = total + cells(coef, i, (3,)) * cells(krylov, i, (k,))
        total = total + cells(coef, i, (4,)) * cells(krylov, i, (k,), 2 * TILE)
        total = total + cells(coef, i, (5,)) * z_low + cells(coef, i, (6,)) * z_high
        return v, total

    row_at = lax.broadcasted_iota(jnp.int32, (TILE, nz), 0)

    def send_sums(k, sums):
        local = none
        for r, value in enumerate(sums):
            local = jnp.where(row_at == r, jnp.sum(value, axis=0, keepdims=True), local)
        red_out[k] = local
        red_in[k, me] = local

        def one(t, carry):
            d = lax.rem(me + t, n)
            pltpu.make_async_remote_copy(
                red_out.at[k],
                red_in.at[k, me],
                red_send.at[k],
                red_recv.at[k],
                device_id=coords(d),
                device_id_type=MESH,
            ).start()
            return carry

        lax.fori_loop(1, n, one, 0)

    def sum_copy(k):
        return pltpu.make_async_remote_copy(
            red_in.at[k, others],
            red_in.at[k, others],
            red_send.at[k],
            red_recv.at[k],
            device_id=coords(lax.rem(me + 1, n)),
            device_id_type=MESH,
        )

    def take_sums(k, count):
        sum_copy(k).wait_recv()
        total = jnp.sum(jnp.sum(red_in[k], axis=0), axis=1, keepdims=True)
        return [jnp.broadcast_to(total[r : r + 1, :], (TILE, nz)) for r in range(count)]

    rim_sets = [send_rims(0)]
    finish_recv(rim_sets[0])

    def first(i, sums):
        v, image = apply_stencil(0, i)
        put(krylov, i, image, (1,), TILE)
        return (sums[0] + fold(v * v), sums[1] + fold(image * v), sums[2] + fold(image * image))

    sums = lax.fori_loop(0, chunks, first, (none, none, none))
    rotations, columns, target = [], [], None
    for j in range(ITERS):
        if j + 1 < ITERS:
            rim_sets.append(send_rims(j + 1))
        send_sums(j, sums)
        if j + 1 < ITERS:
            finish_recv(rim_sets[j + 1])

            def ahead(i, carry):
                put(basis, i, apply_stencil(j + 1, i)[1], (ITERS,))
                return carry

            lax.fori_loop(0, chunks, ahead, 0)
        got = take_sums(j, j + 2 if j else 3)
        if j == 0:
            square = got[0]
            beta = jnp.sqrt(square)
            shrink = 1.0 / beta
            products = [got[1] / square]
            own_square = got[2] / square
            target = [beta] + [none] * ITERS
        else:
            products, own_square = got[: j + 1], got[j + 1]
        rest = own_square
        for value in products:
            rest = rest - value * value
        length = jnp.sqrt(rest)
        column = rotate(products + [length], rotations)
        radius = jnp.sqrt(column[j] * column[j] + column[j + 1] * column[j + 1])
        turn = (column[j] / radius, column[j + 1] / radius)
        column[j] = radius
        rotations.append(turn)
        columns.append(column)
        target[j], target[j + 1] = turn[0] * target[j], -turn[1] * target[j]
        if j + 1 == ITERS:
            break
        inverse_length = 1.0 / length
        if j == 0:
            finish_send(rim_sets[0])

        def advance(i, sums):
            if j == 0:
                low = cells(krylov, i, (0,), TILE) * shrink
                put(basis, i, low, (0,))
                lows = [low]
                images = [cells(krylov, i, (1,), TILE) * shrink]
                put(krylov, i, images[0], (0,), TILE)
                further = cells(basis, i, (ITERS,)) * shrink
            else:
                lows = [cells(basis, i, (k,)) for k in range(j + 1)]
                slots = [0] + list(range(2, j + 2))
                images = [cells(krylov, i, (slot,), TILE) for slot in slots]
                further = cells(basis, i, (ITERS,))
            fresh = images[-1]
            for value, low, image in zip(products, lows, images):
                fresh = fresh - value * low
                further = further - value * image
            fresh = fresh * inverse_length
            further = further * inverse_length
            put(basis, i, fresh, (j + 1,))
            put(krylov, i, further, (j + 2,), TILE)
            lows.append(fresh)
            return tuple(
                s + fold(further * other) for s, other in zip(sums, lows + [further])
            )

        sums = lax.fori_loop(0, chunks, advance, (none,) * (j + 3))

    coeffs = [None] * ITERS
    for j in reversed(range(ITERS)):
        running = target[j]
        for k in range(j + 1, ITERS):
            running = running - columns[k][j] * coeffs[k]
        coeffs[j] = running / columns[j][j]

    def combine(i, carry):
        total = coeffs[0] * cells(basis, i, (0,))
        for k in range(1, ITERS):
            total = total + coeffs[k] * cells(basis, i, (k,))
        put(diag_f, i, total)
        return carry

    lax.fori_loop(0, chunks, combine, 0)
    for x in range(TILE):
        out_ref[pl.ds(x, nz, stride=TILE), :] = diag_f[pl.ds(x, ny, stride=TILE), :].T

    arrival.wait_send()
    finish_send(cond_copies)
    finish_send(level_copies)
    for copies in rim_sets[1:]:
        finish_send(copies)
    for k in range(ITERS):
        sum_copy(k).wait_send()


def body(held_head, held_head_old, material_ids, block_map, conductivity, vg_alpha, vg_n, capacity):
    n_gx, n_gy = lax.axis_size("gx"), lax.axis_size("gy")
    devices = n_gx * n_gy
    own_index = lax.axis_index(("gx", "gy"))
    layers, width, depth = held_head.shape
    slab = layers // devices
    numbers = jnp.arange(devices, dtype=jnp.int32)
    own_row = block_map[own_index]
    send_order = jnp.sum(
        jnp.where(own_row[None, :] == numbers[:, None], numbers[None, :], 0), axis=1
    )
    source_of = jnp.sum(jnp.where(block_map == own_index, numbers[:, None], 0), axis=0)
    order = jnp.stack([send_order, source_of])
    count = layers * width
    padded = (depth + 2) * width
    f32 = jnp.float32
    vmem = pltpu.VMEM
    smem_spec = pl.BlockSpec(memory_space=pltpu.SMEM)
    vmem_spec = pl.BlockSpec(memory_space=pltpu.VMEM)
    plain = vmem((depth * width, layers), f32)
    flat = (count, depth)
    update = pl.pallas_call(
        functools.partial(kernel, n_gx, n_gy, slab),
        out_shape=jax.ShapeDtypeStruct(flat, f32),
        in_specs=[smem_spec] * 5 + [vmem_spec] * 3,
        out_specs=vmem_spec,
        scratch_shapes=[
            vmem((devices, 2 * slab * width, depth), f32),
            vmem((devices, 2 * slab * width, depth), f32),
            vmem((2, count, depth), f32),
            vmem((3, padded, layers), f32),
            plain,
            vmem((padded, layers), f32),
            plain,
            plain,
            plain,
            plain,
            vmem((6, depth * width, layers), f32),
            plain,
            plain,
            vmem((7, depth * width, layers), f32),
            vmem((ITERS + 1, padded, layers), f32),
            vmem((ITERS + 1, depth * width, layers), f32),
            vmem((2, depth, layers), f32),
            vmem((2, depth, layers), f32),
            vmem((2, 3, depth, layers), f32),
            vmem((2, 3, depth, layers), f32),
            vmem((ITERS, 2, depth, layers), f32),
            vmem((ITERS, 2, depth, layers), f32),
            vmem((ITERS, width, layers), f32),
            vmem((ITERS, devices, width, layers), f32),
            pltpu.SemaphoreType.DMA,
            pltpu.SemaphoreType.DMA,
            pltpu.SemaphoreType.DMA((ITERS + 2, 4)),
            pltpu.SemaphoreType.DMA((ITERS + 2, 4)),
            pltpu.SemaphoreType.DMA((ITERS,)),
            pltpu.SemaphoreType.DMA((ITERS,)),
        ],
        compiler_params=pltpu.CompilerParams(
            collective_id=0, has_side_effects=True, vmem_limit_bytes=48 * 1024 * 1024
        ),
    )(
        order,
        conductivity,
        vg_alpha,
        vg_n,
        capacity,
        held_head.reshape(devices, slab * width, depth),
        held_head_old.reshape(devices, slab * width, depth),
        material_ids.reshape(flat),
    )
    return update.reshape(layers, width, depth)


def solution(mesh):
    return jax.shard_map(
        body,
        mesh=mesh,
        in_specs=(
            P(("gx", "gy"), None, None),
            P(("gx", "gy"), None, None),
            P(None, "gx", "gy"),
            P(),
            P(),
            P(),
            P(),
            P(),
        ),
        out_specs=P(None, "gx", "gy"),
        check_vma=False,
    )
```
